512 devices in a mesh: dp: 16 (over y, x), expert: 32 (over z, core).
Axes of the slice: x: 4, y: 4, z: 16, core: 2. Of those that a mesh axis runs over, the one named last changes fastest.
Arguments:
- tokens: bfloat16 [32768, 2048], P(('dp', 'expert')), may hold values from -6 to 6
- route_ids: int32 [32768, 8], P(('dp', 'expert')), may hold values from 0 to 127, all different within a row; in each aligned block of 64 rows (0 to 63, 64 to 127, ...) at most 8 rows name the same one
- route_weights: bfloat16 [32768, 8], P(('dp', 'expert')), may hold values from 0.099609375 to 0.5
- placement: int32 [128], replicated, may hold values from 0 to 127, each once
- gate_proj: bfloat16 [16, 32, 1, 192, 2048], P('dp', 'expert'), may hold values from -0.125 to 0.125
- up_proj: bfloat16 [16, 32, 1, 192, 2048], P('dp', 'expert'), may hold values from -0.125 to 0.125
- down_proj: bfloat16 [16, 32, 1, 192, 2048], P('dp', 'expert'), may hold values from -0.21875 to 0.21875
Outputs:
- mixed: bfloat16 [32768, 2048], P(('dp', 'expert'))
The draws below stay inside these ranges and needn't reach their ends.
Inputs may be any that keep to these rules, and one draw needn't show every extreme that they name: `route_ids`: the 8 ids of a token differ. Among the rows of one device no expert is named more than 8 times, and in every draw some expert is named exactly 8 times by the rows of some device. `placement`: each slot holds exactly one expert.
All inputs are finite; a program needn't handle non-finite values.
Results may differ from the reference program's by a relative error of at most 0.0058.
Values may be sent and summed in bfloat16 or wider, within the bound.
A program may use at most 128 MiB of HBM per device.

```python
import math
import jax
import jax.numpy as jnp
import numpy as np
from jax import lax

D = 2048
FF = 768
E = 128
TOP = 8
TOK_DEV = 64
CAP = 8
SLOTK = 1
QW = 192
TOKENS = 32768
N_DP = 16
N_EXPERT = 32


def steps_of(key, extent, pieces, low, top_value):
    factor_of, own = 1.0, jax.random.fold_in(key, 6)
    for dim, shards_of in pieces:
        heights = jnp.exp(jax.random.uniform(jax.random.fold_in(own, dim), (shards_of,), jnp.float32, low / len(pieces), top_value / len(pieces)))
        factor_of = factor_of * jnp.repeat(heights, extent[dim] // shards_of).reshape([-1 if axis == dim else 1 for axis in range(len(extent))])
    return factor_of


def shared_out(stream_key, own, number, rows, count, top, bound, slope):
    ranking = jax.random.permutation(stream_key, count)
    packed, ordinary = portions_of(count, rows * top, bound, slope, True), portions_of(count, rows * top, bound, slope, False)
    places = jnp.arange(count)

    def named(sizes, rotation):
        used = int((sizes > 0).sum())
        fixed = max(1, used // 4)
        passed = fixed + (places - fixed + rotation * (used - fixed)) % max(1, count - fixed)
        return jnp.zeros((count,), jnp.int32).at[ranking[jnp.where(places < fixed, places, passed)]].set(jnp.asarray(sizes, jnp.int32))

    sizes = jnp.where(number % 4 == 0, named(packed, number // 4), named(ordinary, number - number // 4 - 1))
    mixed = jax.random.permutation(jax.random.fold_in(own, 3), count)
    giver, receiver = mixed[0:count // 2 * 2:2], mixed[1:count // 2 * 2:2]
    slack = jnp.minimum(sizes[giver] - 1, bound - sizes[receiver]) // 2
    slack = jnp.where((giver == ranking[0]) | (receiver == ranking[0]) | (sizes[receiver] == 0), 0, jnp.maximum(slack, 0))
    passed = jax.random.randint(jax.random.fold_in(own, 4), (count // 2,), 0, 1 << 20) % (slack + 1)
    sizes = sizes.at[giver].add(-passed).at[receiver].add(passed)
    labels = jnp.searchsorted(jnp.cumsum(sizes), jnp.arange(rows * top), side="right").astype(jnp.int32)
    listing = labels.reshape(top, rows).T
    listing = listing[jax.random.permutation(jax.random.fold_in(own, 1), rows)]
    rotation = jax.random.randint(jax.random.fold_in(own, 2), (rows, 1), 0, top)
    return jnp.take_along_axis(listing, (jnp.arange(top)[None, :] + rotation) % top, axis=1)


def portions_of(amount, total, reach, skew, full):
    portions = [(1 << 20) // math.isqrt(rank ** skew) + 1 for rank in range(1, amount + 1)]
    largest = reach if full else min(reach, max(-(-total // amount), total * portions[0] // sum(portions)))
    least = 1 if total - largest >= amount - 1 else 0
    counts, rest = [largest] + [least] * (amount - 1), total - largest - least * (amount - 1)
    while rest > 0:
        movable = [i for i in range(1, amount) if counts[i] < largest] or [i for i in range(1, amount) if counts[i] < reach]
        whole, left = sum([portions[i] for i in movable]), rest
        for i in movable:
            more = min(reach - counts[i], max(1, left * portions[i] // whole), rest)
            counts[i] = counts[i] + more
            rest = rest - more
    return np.array(counts)


def noise(key, shape, spread, limit, split=(), kind=jnp.bfloat16):
    loudness = steps_of(key, shape, split, -0.22, 0.18) if split else 1.0
    result = jax.random.normal(key, shape, jnp.float32) * spread * loudness
    return jnp.minimum(jnp.maximum(result, -limit), limit).astype(kind)


def setup_inputs(seed: int = 0) -> dict:
    seeds = jax.random.split(jax.random.key(seed), 8)
    tokens = noise(seeds[0], (TOKENS, D), 1.0, 6.0, ((0, 512),))
    route_ids_keys = jax.random.split(jax.random.fold_in(seeds[1], 1), TOKENS // TOK_DEV)
    route_ids_turns = jax.random.permutation(jax.random.fold_in(seeds[1], 3), TOKENS // TOK_DEV)
    route_ids = jax.vmap(lambda own, number: shared_out(jax.random.fold_in(seeds[1], 2), own, number, TOK_DEV, E, TOP, CAP, 2))(route_ids_keys, route_ids_turns).reshape((TOKENS, TOP))
    route_weights = jnp.clip(0.099609375 + 0.40039062 * jax.random.uniform(seeds[2], (TOKENS, TOP), jnp.float32) ** steps_of(seeds[2], (TOKENS, TOP), ((0, 512),), -0.2, 0.2), 0.099609375, 0.5).astype(jnp.bfloat16)
    placement = jax.random.permutation(seeds[3], E).astype(jnp.int32)
    gate_proj = noise(seeds[4], (N_DP, N_EXPERT, SLOTK, QW, D), D ** -0.5, 0.125, ((0, 16), (1, 32)))
    up_proj = noise(seeds[5], (N_DP, N_EXPERT, SLOTK, QW, D), D ** -0.5, 0.125, ((0, 16), (1, 32)))
    down_proj = noise(seeds[6], (N_DP, N_EXPERT, SLOTK, QW, D), FF ** -0.5, 0.21875, ((0, 16), (1, 32)))
    return {"tokens": tokens, "route_ids": route_ids, "route_weights": route_weights, "placement": placement, "gate_proj": gate_proj, "up_proj": up_proj, "down_proj": down_proj}


def reference(tokens, route_ids, route_weights, placement, gate_proj, up_proj, down_proj):
    devices = N_DP * N_EXPERT
    groups = N_EXPERT // 4
    per_slot = gate_proj.shape[2]
    hot = (route_ids[:, :, None] == jnp.arange(E, dtype=jnp.int32)[None, None, :]).astype(jnp.int32)
    blocks = hot.reshape(devices, TOK_DEV * TOP, E)
    earlier = jnp.cumsum(blocks, axis=1) - blocks
    position = jnp.sum(earlier * blocks, axis=2).reshape(TOKENS, TOP).astype(jnp.int32)
    token_index = jnp.broadcast_to(jnp.arange(TOKENS, dtype=jnp.int32)[:, None], (TOKENS, TOP))
    device_index = (token_index // TOK_DEV).astype(jnp.int32)
    tok_table = jnp.full((E, devices, CAP), TOKENS, jnp.int32).at[route_ids, device_index, position].set(token_index)
    weight_table = jnp.zeros((E, devices, CAP), jnp.float32).at[route_ids, device_index, position].set(route_weights.astype(jnp.float32))
    padded = jnp.concatenate([tokens, jnp.zeros((1, D), tokens.dtype)], axis=0)
    zero = jnp.zeros((), jnp.int32)

    def step(total, expert):
        slot = placement[expert].astype(jnp.int32)
        row = (slot // (groups * per_slot)).astype(jnp.int32)
        group = ((slot // per_slot) % groups).astype(jnp.int32)
        inner = (slot % per_slot).astype(jnp.int32)
        starts = (row, group * 4, inner, zero, zero)
        gate_w = lax.dynamic_slice(gate_proj, starts, (1, 4, 1, QW, D)).reshape(FF, D)
        up_w = lax.dynamic_slice(up_proj, starts, (1, 4, 1, QW, D)).reshape(FF, D)
        down_w = lax.dynamic_slice(down_proj, starts, (1, 4, 1, QW, D)).reshape(FF, D)
        index = tok_table[expert].reshape(-1)
        rows = padded[index]
        gate = jnp.dot(rows, gate_w.T, preferred_element_type=jnp.float32)
        up = jnp.dot(rows, up_w.T, preferred_element_type=jnp.float32)
        hidden = (jax.nn.silu(gate) * up).astype(jnp.bfloat16)
        out_rows = jnp.dot(hidden, down_w, preferred_element_type=jnp.float32).astype(jnp.bfloat16)
        weights = weight_table[expert].reshape(-1)
        total = total.at[index].add(weights[:, None] * out_rows.astype(jnp.float32))
        return total, None

    total, _ = lax.scan(step, jnp.zeros((TOKENS + 1, D), jnp.float32), jnp.arange(E, dtype=jnp.int32))
    return total[:TOKENS].astype(jnp.bfloat16)
```

```python
import functools

import jax
import jax.numpy as jnp
from jax import lax
from jax.experimental import pallas as pl
from jax.experimental.pallas import tpu as pltpu
from jax.sharding import PartitionSpec as P

CAP = 8
BF = jnp.bfloat16
F32 = jnp.float32
MESH = pl.DeviceIdType.MESH
RING = 8


def nt(a, b):
    return lax.dot_general(a, b, (((1,), (1,)), ((), ())), preferred_element_type=F32)


def nn(a, b):
    return lax.dot_general(a, b, (((1,), (0,)), ((), ())), preferred_element_type=F32)


def tn(a, b):
    return lax.dot_general(a, b, (((0,), (0,)), ((), ())), preferred_element_type=F32)


def iota(shape, dim):
    return lax.broadcasted_iota(jnp.int32, shape, dim)


def kernel(
    n_rows, ids_ref, wts_ref, place_ref, tok_ref, gate_hbm, up_hbm, down_hbm, out_ref,
    tok, meta_out, meta, disp, arr, yout, ret, stage, rsum, gw, uw, dw, hid,
    tok_send, tok_recv, meta_send, meta_recv, disp_send, arr_recv, y_send, ret_recv,
    rs_send, rs_recv, w_local, w_send, w_cross, w_sib, w_diag,
):
    tokens, width = tok_ref.shape
    half = tokens // 2
    quarter = gate_hbm.shape[3]
    experts = place_ref.shape[1]
    topk = ids_ref.shape[1]
    slots = n_rows * CAP
    row = lax.axis_index("dp")
    col = lax.axis_index("expert")
    g = lax.div(col, 4)
    q = lax.rem(col, 4)

    def ring(step):
        return (row, lax.rem(g + RING + step, RING) * 4 + q)

    sibling = (row, g * 4 + q + 1 - 2 * lax.rem(q, 2))
    cross = (row, g * 4 + lax.rem(q + 2, 4))

    def plane(step):
        return lax.rem(row + step, n_rows)

    def remote(src, dst, send, recv, device):
        return pltpu.make_async_remote_copy(
            src_ref=src, dst_ref=dst, send_sem=send, recv_sem=recv,
            device_id=device, device_id_type=MESH,
        )

    def wait_for(ref, sem):
        pltpu.make_async_copy(ref, ref, sem).wait()

    barrier = pltpu.get_barrier_semaphore()
    partners = [ring(d) for d in range(1, RING)] + [sibling, cross]
    partners += [(plane(j), col) for j in range(1, n_rows)]
    for device in partners:
        pl.semaphore_signal(barrier, inc=1, device_id=device, device_id_type=MESH)

    weights = ((gate_hbm, gw), (up_hbm, uw), (down_hbm, dw))
    for n, (src, dst) in enumerate(weights):
        pltpu.make_async_copy(src.at[0, 0, 0], dst.at[pl.ds(0, quarter)], w_local.at[n]).start()

    lane = iota((tokens, experts), 1)
    hot = jnp.zeros((tokens, experts), F32)
    mix = jnp.zeros((tokens, experts), F32)
    for j in range(topk):
        same = ids_ref[:, j : j + 1] == lane
        hot = hot + jnp.where(same, 1.0, 0.0)
        mix = mix + jnp.where(same, wts_ref[:, j : j + 1], 0.0)
    below = jnp.where(iota((tokens, tokens), 1) < iota((tokens, tokens), 0), 1.0, 0.0).astype(BF)
    earlier = nn(below, hot.astype(BF))
    both = jnp.concatenate([hot * (earlier + 1.0), mix], axis=0).astype(BF)
    order = iota((experts, experts), 0)
    slot_of = lax.rem(order, n_rows) * RING + lax.div(order, n_rows)
    pick = jnp.where(place_ref[...] == slot_of, 1.0, 0.0).astype(BF)
    spread = nt(pick, both)
    meta_out[...] = spread.reshape(RING, n_rows, 2 * tokens)
    tok[0] = tok_ref[...]
    rsum[6, half:] = jnp.zeros((half, width), BF)
    rsum[7, :half] = jnp.zeros((half, width), BF)

    pl.semaphore_wait(barrier, len(partners))

    own_up = remote(tok.at[0], tok.at[1], tok_send.at[0], tok_recv.at[1], ring(1))
    own_down = remote(tok.at[0], tok.at[2], tok_send.at[7], tok_recv.at[2], ring(-1))
    meta_copies = []
    for slot, step in ((1, 1), (2, -1), (3, 2), (4, -2), (5, 3), (6, -3), (7, 4)):
        there = lax.rem(g + RING + step, RING)
        meta_copies.append(
            remote(meta_out.at[there], meta.at[slot], meta_send.at[slot], meta_recv.at[slot], ring(step))
        )
    for copy in meta_copies:
        copy.start()
    own_up.start()
    own_down.start()
    meta[0] = meta_out[g]
    cross_copies = [
        remote(src.at[0, 0, 0], dst.at[pl.ds(2 * quarter, quarter)], w_send.at[n], w_cross.at[n], cross)
        for n, (src, dst) in enumerate(weights)
    ]
    sib_copies = [
        remote(src.at[0, 0, 0], dst.at[pl.ds(quarter, quarter)], w_send.at[3 + n], w_sib.at[n], sibling)
        for n, (src, dst) in enumerate(weights)
    ]
    diag_copies = [
        remote(dst.at[pl.ds(2 * quarter, quarter)], dst.at[pl.ds(3 * quarter, quarter)], w_send.at[6 + n], w_diag.at[n], sibling)
        for n, (_, dst) in enumerate(weights)
    ]
    for copy in cross_copies + sib_copies:
        copy.start()

    grow = jnp.where(lax.div(iota((slots, n_rows), 0), CAP) == iota((slots, n_rows), 1), 1.0, 0.0)
    place_in = (lax.rem(iota((slots, tokens), 0), CAP) + 1).astype(F32)

    def send_rows(i, src, dst, send, recv):
        pltpu.make_async_copy(src.at[i, row], dst.at[i, row], recv.at[i]).start()
        for j in range(1, n_rows):
            there = plane(j)
            remote(src.at[i, there], dst.at[i, row], send.at[i], recv.at[i], (there, col)).start()

    wide = min(512, width)

    def dispatch(i, _):
        @pl.when(i > 0)
        def _():
            wait_for(tok.at[i], tok_recv.at[i])
            wait_for(meta.at[i], meta_recv.at[i])

        @pl.when((i >= 1) & (i <= 4))
        def _():
            remote(tok.at[i], tok.at[i + 2], tok_send.at[i], tok_recv.at[i + 2], ring(2 * lax.rem(i, 2) - 1)).start()

        @pl.when(i == 5)
        def _():
            remote(tok.at[5, pl.ds(0, half)], tok.at[7, pl.ds(0, half)], tok_send.at[5], tok_recv.at[7], ring(1)).start()

        @pl.when(i == 6)
        def _():
            remote(tok.at[6, pl.ds(half, half)], tok.at[7, pl.ds(half, half)], tok_send.at[6], tok_recv.at[7], ring(-1)).start()

        grown = nn(grow, meta[i])
        hot_rows = jnp.where(grown[:, :tokens] == place_in, 1.0, 0.0).astype(BF)
        for n in range(0, width, wide):
            rows = nn(hot_rows, tok[i, :, n : n + wide])
            disp[i, :, :, n : n + wide] = rows.reshape(n_rows, CAP, wide).astype(BF)
        send_rows(i, disp, arr, disp_send, arr_recv)
        return 0

    lax.fori_loop(0, RING, dispatch, 0)

    for n, (src, dst) in enumerate(weights):
        cross_copies[n].wait_recv()
        diag_copies[n].start()
    for n, (src, dst) in enumerate(weights):
        pltpu.make_async_copy(src.at[0, 0, 0], dst.at[pl.ds(0, quarter)], w_local.at[n]).wait()
        sib_copies[n].wait_recv()
        diag_copies[n].wait_recv()

    hidden = gw.shape[0]
    tile = hidden // 3

    def expert(k, _):
        i = RING - 1 - k
        wait_for(arr.at[i], arr_recv.at[i])
        x = arr[i].astype(F32).reshape(slots, width).astype(BF)
        for h in range(0, hidden, tile):
            gate = nt(x, gw[h : h + tile, :])
            up = nt(x, uw[h : h + tile, :])
            hid[:, h : h + tile] = (gate / (1.0 + jnp.exp(-gate)) * up).astype(BF)
        for n in range(0, width, wide):
            y = nn(hid[...], dw[:, n : n + wide])
            yout[i, :, :, n : n + wide] = y.reshape(n_rows, CAP, wide).astype(BF)
        send_rows(i, yout, ret, y_send, ret_recv)
        return 0

    lax.fori_loop(0, RING, expert, 0)

    def mixing(i):
        wait_for(ret.at[i], ret_recv.at[i])
        grown = nn(grow, meta[i])
        return jnp.where(grown[:, :tokens] == place_in, grown[:, tokens:], 0.0).astype(BF)

    def part(i, mixer, n):
        rows = ret[i, :, :, n : n + wide].astype(F32).reshape(slots, wide).astype(BF)
        return tn(mixer, rows)

    mixer = mixing(7)
    for n in range(0, width, wide):
        stage[7, :, n : n + wide] = part(7, mixer, n).astype(BF)
    far = (
        remote(stage.at[7, pl.ds(0, half)], rsum.at[6, pl.ds(0, half)], rs_send.at[7], rs_recv.at[6], ring(-1)),
        remote(stage.at[7, pl.ds(half, half)], rsum.at[7, pl.ds(half, half)], rs_send.at[0], rs_recv.at[7], ring(1)),
    )
    for copy in far:
        copy.start()

    def reduce(k, _):
        i = 6 - k
        mixer = mixing(i)

        @pl.when(i >= 5)
        def _():
            wait_for(rsum.at[i + 1, pl.ds(0, half)], rs_recv.at[i + 1])

        @pl.when(i <= 4)
        def _():
            wait_for(rsum.at[i + 1], rs_recv.at[i + 1])

        for n in range(0, width, wide):
            total = part(i, mixer, n) + rsum[i + 1, :, n : n + wide].astype(F32)
            stage[i, :, n : n + wide] = total.astype(BF)
        remote(stage.at[i], rsum.at[i - 1], rs_send.at[i], rs_recv.at[i - 1], ring(1 - 2 * lax.rem(i, 2))).start()
        return 0

    lax.fori_loop(0, 6, reduce, 0)

    mixer = mixing(0)
    wait_for(rsum.at[0], rs_recv.at[0])
    wait_for(rsum.at[1], rs_recv.at[1])
    for n in range(0, width, wide):
        near = rsum[0, :, n : n + wide].astype(F32) + rsum[1, :, n : n + wide].astype(F32)
        out_ref[:, n : n + wide] = (part(0, mixer, n) + near).astype(BF)

    own_up.wait_send()
    own_down.wait_send()
    for copy in meta_copies + cross_copies + sib_copies + diag_copies:
        copy.wait_send()
    for copy in far:
        copy.wait_send()

    def drain(i, _):
        wait_for(disp.at[i, pl.ds(0, n_rows - 1)], disp_send.at[i])
        wait_for(yout.at[i, pl.ds(0, n_rows - 1)], y_send.at[i])

        @pl.when((i >= 1) & (i <= 4))
        def _():
            wait_for(tok.at[i], tok_send.at[i])

        @pl.when((i == 5) | (i == 6))
        def _():
            wait_for(tok.at[i, pl.ds(0, half)], tok_send.at[i])

        @pl.when((i >= 1) & (i <= 6))
        def _():
            wait_for(stage.at[i], rs_send.at[i])

        return 0

    lax.fori_loop(0, RING, drain, 0)


def on_device(n_rows, tokens, route_ids, route_weights, placement, gate_proj, up_proj, down_proj):
    count, width = tokens.shape
    quarter = gate_proj.shape[3]
    experts = placement.shape[0]
    blocks = (RING, n_rows, CAP, width)
    vmem = pl.BlockSpec(memory_space=pltpu.VMEM)
    hbm = pl.BlockSpec(memory_space=pl.ANY)
    dma = pltpu.SemaphoreType.DMA
    scratch = [
        pltpu.VMEM((RING, count, width), BF),
        pltpu.VMEM((RING, n_rows, 2 * count), F32),
        pltpu.VMEM((RING, n_rows, 2 * count), F32),
        pltpu.VMEM(blocks, BF),
        pltpu.VMEM(blocks, BF),
        pltpu.VMEM(blocks, BF),
        pltpu.VMEM(blocks, BF),
        pltpu.VMEM((RING, count, width), BF),
        pltpu.VMEM((RING, count, width), BF),
        pltpu.VMEM((4 * quarter, width), BF),
        pltpu.VMEM((4 * quarter, width), BF),
        pltpu.VMEM((4 * quarter, width), BF),
        pltpu.VMEM((n_rows * CAP, 4 * quarter), BF),
    ]
    scratch += [dma((RING,)) for _ in range(10)]
    scratch += [dma((3,)), dma((9,)), dma((3,)), dma((3,)), dma((3,))]
    return pl.pallas_call(
        functools.partial(kernel, n_rows),
        out_shape=jax.ShapeDtypeStruct((count, width), BF),
        in_specs=[vmem, vmem, vmem, vmem, hbm, hbm, hbm],
        out_specs=vmem,
        scratch_shapes=scratch,
        compiler_params=pltpu.CompilerParams(
            collective_id=0, has_side_effects=True, vmem_limit_bytes=60 * 2**20
        ),
    )(
        route_ids,
        route_weights.astype(F32),
        placement.reshape(1, experts),
        tokens,
        gate_proj,
        up_proj,
        down_proj,
    )


def solution(mesh):
    in_specs = (
        P(("dp", "expert"), None),
        P(("dp", "expert"), None),
        P(("dp", "expert"), None),
        P(),
        P("dp", "expert", None, None, None),
        P("dp", "expert", None, None, None),
        P("dp", "expert", None, None, None),
    )
    return jax.shard_map(
        functools.partial(on_device, mesh.shape["dp"]),
        mesh=mesh,
        in_specs=in_specs,
        out_specs=P(("dp", "expert"), None),
        check_vma=False,
    )
```

```python
import functools

import jax
import jax.numpy as jnp
from jax import lax
from jax.experimental import pallas as pl
from jax.experimental.pallas import tpu as pltpu
from jax.sharding import PartitionSpec as P

CAP = 8
BF = jnp.bfloat16
F32 = jnp.float32
MESH = pl.DeviceIdType.MESH
RING = 8


def nt(a, b):
    return lax.dot_general(a, b, (((1,), (1,)), ((), ())), preferred_element_type=F32)


def nn(a, b):
    return lax.dot_general(a, b, (((1,), (0,)), ((), ())), preferred_element_type=F32)


def tn(a, b):
    return lax.dot_general(a, b, (((0,), (0,)), ((), ())), preferred_element_type=F32)


def iota(shape, dim):
    return lax.broadcasted_iota(jnp.int32, shape, dim)


def kernel(
    n_rows, ids_ref, wts_ref, place_ref, tok_ref, gate_hbm, up_hbm, down_hbm, out_ref,
    tok, meta_out, meta, disp, arr, yout, ret, stage, rsum, gw, uw, dw, hid,
    tok_send, tok_recv, meta_send, meta_recv, disp_send, arr_recv, y_send, ret_recv,
    rs_send, rs_recv, w_local, w_send, w_cross, w_sib, w_diag,
):
    tokens, width = tok_ref.shape
    quarter = gate_hbm.shape[3]
    experts = place_ref.shape[1]
    topk = ids_ref.shape[0]
    slots = n_rows * CAP
    row = lax.axis_index("dp")
    col = lax.axis_index("expert")
    g = lax.div(col, 4)
    q = lax.rem(col, 4)

    way = 1 - 2 * lax.div(q, 2)
    facing = lax.rem(q + 2, 4)

    def ring(step, part):
        return (row, lax.rem(g + RING + way * step, RING) * 4 + part)

    down = ring(1, q)
    up = ring(-1, q)
    across = ring(-1, facing)
    readers = [(d, part) for d in (1, 2, 3) for part in (0, 1)] + [(4, 0)]

    def reader(d, part):
        return ring(-d, facing) if part else ring(d, q)

    sibling = (row, g * 4 + q + 1 - 2 * lax.rem(q, 2))
    cross = (row, g * 4 + facing)

    def plane(step):
        return lax.rem(row + step, n_rows)

    def remote(src, dst, send, recv, device):
        return pltpu.make_async_remote_copy(
            src_ref=src, dst_ref=dst, send_sem=send, recv_sem=recv,
            device_id=device, device_id_type=MESH,
        )

    def wait_for(ref, sem):
        pltpu.make_async_copy(ref, ref, sem).wait()

    barrier = pltpu.get_barrier_semaphore()
    partners = [reader(d, part) for d, part in readers]
    partners += [ring(-d, q) for d in (1, 2, 3)]
    partners += [sibling, cross]
    partners += [(plane(j), col) for j in range(1, n_rows)]
    for device in partners:
        pl.semaphore_signal(barrier, inc=1, device_id=device, device_id_type=MESH)

    weights = ((gate_hbm, gw), (up_hbm, uw), (down_hbm, dw))
    for n, (src, dst) in enumerate(weights):
        pltpu.make_async_copy(src.at[0, 0, 0], dst.at[pl.ds(0, quarter)], w_local.at[n]).start()

    name = iota((experts, tokens), 0)
    hot = jnp.zeros((experts, tokens), F32)
    mix = jnp.zeros((experts, tokens), F32)
    for j in range(topk):
        same = ids_ref[j : j + 1, :] == name
        hot = hot + jnp.where(same, 1.0, 0.0)
        mix = mix + jnp.where(same, wts_ref[j : j + 1, :].astype(F32), 0.0)
    before = jnp.where(iota((tokens, tokens), 0) < iota((tokens, tokens), 1), 1.0, 0.0).astype(BF)
    earlier = nn(hot.astype(BF), before)
    order = iota((experts, experts), 0)
    slot_of = lax.rem(order, n_rows) * RING + lax.div(order, n_rows)
    pick = jnp.where(place_ref[...] == slot_of, 1.0, 0.0).astype(BF)
    place_to = nn(pick, (hot * (earlier + 1.0)).astype(BF))
    meta_out[:, :, :tokens] = place_to.reshape(RING, n_rows, tokens)
    meta_out[:, :, tokens:] = nn(pick, mix.astype(BF)).reshape(RING, n_rows, tokens)
    tok[0] = tok_ref[...]

    pl.semaphore_wait(barrier, len(partners))

    own_copies = [
        remote(tok.at[0], tok.at[1], tok_send.at[0], tok_recv.at[1], down),
        remote(tok.at[0], tok.at[2], tok_send.at[7], tok_recv.at[2], across),
    ]
    meta_copies = []
    for slot, (d, part) in enumerate(readers, 1):
        there = lax.rem(g + RING + way * (-d if part else d), RING)
        meta_copies.append(
            remote(meta_out.at[there], meta.at[slot], meta_send.at[slot], meta_recv.at[slot], reader(d, part))
        )
    for copy in meta_copies + own_copies:
        copy.start()
    meta[0] = meta_out[g]
    piece = quarter // 2

    def moved(dst, source, n, to):
        return dst.at[pl.ds(to * quarter + n * piece, piece)] if source is None else source.at[0, 0, 0, pl.ds(n * piece, piece)]

    cross_copies, sib_copies, diag_copies = [], [], []
    for w, (src, dst) in enumerate(weights):
        for n in range(2):
            k = 2 * w + n
            mine = moved(dst, src, n, 0)
            cross_copies.append(remote(mine, moved(dst, None, n, 2), w_send.at[k], w_cross.at[k], cross))
            sib_copies.append(remote(mine, moved(dst, None, n, 1), w_send.at[6 + k], w_sib.at[k], sibling))
            diag_copies.append(
                remote(moved(dst, None, n, 2), moved(dst, None, n, 3), w_send.at[12 + k], w_diag.at[k], sibling)
            )

    grow = jnp.where(lax.div(iota((slots, n_rows), 0), CAP) == iota((slots, n_rows), 1), 1.0, 0.0)
    place_in = (lax.rem(iota((slots, tokens), 0), CAP) + 1).astype(F32)

    def send_rows(i, src, dst, send, recv):
        pltpu.make_async_copy(src.at[i, row], dst.at[i, row], recv.at[i]).start()
        for j in range(1, n_rows):
            there = plane(j)
            remote(src.at[i, there], dst.at[i, row], send.at[i], recv.at[i], (there, col)).start()

    wide = min(512, width)

    def dispatch(i, _):
        @pl.when(i > 0)
        def _():
            wait_for(tok.at[i], tok_recv.at[i])
            wait_for(meta.at[i], meta_recv.at[i])

        @pl.when((i >= 1) & (i <= 5))
        def _():
            remote(tok.at[i], tok.at[i + 2], tok_send.at[i], tok_recv.at[i + 2], down).start()

        @pl.when(i == 5)
        def _():
            for copy in cross_copies + sib_copies:
                copy.start()

        grown = nn(grow, meta[i])
        hot_rows = jnp.where(grown[:, :tokens] == place_in, 1.0, 0.0).astype(BF)
        for n in range(0, width, wide):
            rows = nn(hot_rows, tok[i, :, n : n + wide])
            disp[i, :, :, n : n + wide] = rows.reshape(n_rows, CAP, wide).astype(BF)
        send_rows(i, disp, arr, disp_send, arr_recv)
        return 0

    lax.fori_loop(0, RING, dispatch, 0)

    def take(n):
        for k in range(2 * n, 2 * n + 2):
            cross_copies[k].wait_recv()
            diag_copies[k].start()

    def have(n):
        src, dst = weights[n]
        pltpu.make_async_copy(src.at[0, 0, 0], dst.at[pl.ds(0, quarter)], w_local.at[n]).wait()
        for k in range(2 * n, 2 * n + 2):
            sib_copies[k].wait_recv()
            diag_copies[k].wait_recv()

    hidden = gw.shape[0]
    tile = hidden // 3

    def gated(k, _):
        wait_for(arr.at[2 * k], arr_recv.at[2 * k])
        wait_for(arr.at[2 * k + 1], arr_recv.at[2 * k + 1])
        x = arr[pl.ds(2 * k, 2)].astype(F32).reshape(2 * slots, width).astype(BF)
        for h in range(0, hidden, tile):
            gate = nt(x, gw[h : h + tile, :])
            up = nt(x, uw[h : h + tile, :])
            kept = (gate / (1.0 + jnp.exp(-gate)) * up).astype(BF)
            hid[pl.ds(2 * k, 2), :, h : h + tile] = kept.reshape(2, slots, tile)
        return 0

    def projected(k, _):
        i = RING - 1 - k
        for n in range(0, width, wide):
            y = nn(hid[i], dw[:, n : n + wide])
            yout[i, :, :, n : n + wide] = y.reshape(n_rows, CAP, wide).astype(BF)
        send_rows(i, yout, ret, y_send, ret_recv)
        return 0

    take(0)
    take(1)
    have(0)
    have(1)
    lax.fori_loop(0, RING // 2, gated, 0)
    take(2)
    have(2)
    lax.fori_loop(0, RING, projected, 0)

    def mixing(i):
        wait_for(ret.at[i], ret_recv.at[i])
        grown = nn(grow, meta[i])
        return jnp.where(grown[:, :tokens] == place_in, grown[:, tokens:], 0.0).astype(BF)

    def part(i, mixer, n):
        rows = ret[i, :, :, n : n + wide].astype(F32).reshape(slots, wide).astype(BF)
        return tn(mixer, rows)

    def reduce(k, _):
        i = RING - 1 - k
        mixer = mixing(i)

        @pl.when(i <= 5)
        def _():
            wait_for(rsum.at[i + 1], rs_recv.at[i + 1])
            for n in range(0, width, wide):
                total = part(i, mixer, n) + rsum[i + 1, :, n : n + wide].astype(F32)
                stage[i, :, n : n + wide] = total.astype(BF)

        @pl.when(i > 5)
        def _():
            for n in range(0, width, wide):
                stage[i, :, n : n + wide] = part(i, mixer, n).astype(BF)

        @pl.when(i != 2)
        def _():
            remote(stage.at[i], rsum.at[i - 1], rs_send.at[i], rs_recv.at[i - 1], up).start()

        @pl.when(i == 2)
        def _():
            remote(stage.at[2], rsum.at[1], rs_send.at[2], rs_recv.at[1], across).start()

        return 0

    lax.fori_loop(0, RING - 1, reduce, 0)

    mixer = mixing(0)
    wait_for(rsum.at[0], rs_recv.at[0])
    wait_for(rsum.at[1], rs_recv.at[1])
    for n in range(0, width, wide):
        near = rsum[0, :, n : n + wide].astype(F32) + rsum[1, :, n : n + wide].astype(F32)
        out_ref[:, n : n + wide] = (part(0, mixer, n) + near).astype(BF)

    for copy in own_copies + meta_copies + cross_copies + sib_copies + diag_copies:
        copy.wait_send()

    def drain(i, _):
        wait_for(disp.at[i, pl.ds(0, n_rows - 1)], disp_send.at[i])
        wait_for(yout.at[i, pl.ds(0, n_rows - 1)], y_send.at[i])

        @pl.when((i >= 1) & (i <= 5))
        def _():
            wait_for(tok.at[i], tok_send.at[i])

        @pl.when(i >= 1)
        def _():
            wait_for(stage.at[i], rs_send.at[i])

        return 0

    lax.fori_loop(0, RING, drain, 0)


def on_device(n_rows, tokens, route_ids, route_weights, placement, gate_proj, up_proj, down_proj):
    count, width = tokens.shape
    quarter = gate_proj.shape[3]
    experts = placement.shape[0]
    blocks = (RING, n_rows, CAP, width)
    vmem = pl.BlockSpec(memory_space=pltpu.VMEM)
    hbm = pl.BlockSpec(memory_space=pl.ANY)
    dma = pltpu.SemaphoreType.DMA
    scratch = [
        pltpu.VMEM((RING, count, width), BF),
        pltpu.VMEM((RING, n_rows, 2 * count), F32),
        pltpu.VMEM((RING, n_rows, 2 * count), F32),
        pltpu.VMEM(blocks, BF),
        pltpu.VMEM(blocks, BF),
        pltpu.VMEM(blocks, BF),
        pltpu.VMEM(blocks, BF),
        pltpu.VMEM((RING, count, width), BF),
        pltpu.VMEM((RING, count, width), BF),
        pltpu.VMEM((4 * quarter, width), BF),
        pltpu.VMEM((4 * quarter, width), BF),
        pltpu.VMEM((4 * quarter, width), BF),
        pltpu.VMEM((RING, n_rows * CAP, 4 * quarter), BF),
    ]
    scratch += [dma((RING,)) for _ in range(10)]
    scratch += [dma((3,)), dma((18,)), dma((6,)), dma((6,)), dma((6,))]
    return pl.pallas_call(
        functools.partial(kernel, n_rows),
        out_shape=jax.ShapeDtypeStruct((count, width), BF),
        in_specs=[vmem, vmem, vmem, vmem, hbm, hbm, hbm],
        out_specs=vmem,
        scratch_shapes=scratch,
        compiler_params=pltpu.CompilerParams(
            collective_id=0, has_side_effects=True, vmem_limit_bytes=60 * 2**20
        ),
    )(
        route_ids.T,
        route_weights.T,
        placement.reshape(1, experts),
        tokens,
        gate_proj,
        up_proj,
        down_proj,
    )


def solution(mesh):
    in_specs = (
        P(("dp", "expert"), None),
        P(("dp", "expert"), None),
        P(("dp", "expert"), None),
        P(),
        P("dp", "expert", None, None, None),
        P("dp", "expert", None, None, None),
        P("dp", "expert", None, None, None),
    )
    return jax.shard_map(
        functools.partial(on_device, mesh.shape["dp"]),
        mesh=mesh,
        in_specs=in_specs,
        out_specs=P(("dp", "expert"), None),
        check_vma=False,
    )
```

```python
import functools

import jax
import jax.numpy as jnp
from jax import lax
from jax.experimental import pallas as pl
from jax.experimental.pallas import tpu as pltpu
from jax.sharding import PartitionSpec as P

CAP = 8
BF = jnp.bfloat16
F32 = jnp.float32
MESH = pl.DeviceIdType.MESH
RING = 8


def nt(a, b):
    return lax.dot_general(a, b, (((1,), (1,)), ((), ())), preferred_element_type=F32)


def nn(a, b):
    return lax.dot_general(a, b, (((1,), (0,)), ((), ())), preferred_element_type=F32)


def tn(a, b):
    return lax.dot_general(a, b, (((0,), (0,)), ((), ())), preferred_element_type=F32)


def iota(shape, dim):
    return lax.broadcasted_iota(jnp.int32, shape, dim)


def kernel(
    n_rows, ids_ref, wts_ref, place_ref, tok_ref, gate_hbm, up_hbm, down_hbm, out_ref,
    tok, meta_out, meta, disp, arr, yout, ret, stage, rsum, gw, uw, dw, hid,
    tok_send, tok_recv, meta_send, meta_recv, disp_send, arr_recv, y_send, ret_recv,
    rs_send, rs_recv, w_local, w_send, w_cross, w_sib, w_diag,
):
    tokens, width = tok_ref.shape
    quarter = gate_hbm.shape[3]
    experts = place_ref.shape[1]
    topk = ids_ref.shape[0]
    slots = n_rows * CAP
    row = lax.axis_index("dp")
    col = lax.axis_index("expert")
    g = lax.div(col, 4)
    q = lax.rem(col, 4)

    way = 1 - 2 * lax.div(q, 2)
    facing = lax.rem(q + 2, 4)

    def ring(step, part):
        return (row, lax.rem(g + RING + way * step, RING) * 4 + part)

    down = ring(1, q)
    up = ring(-1, q)
    across = ring(-1, facing)
    readers = [(d, part) for d in (1, 2, 3) for part in (0, 1)] + [(4, 0)]

    def reader(d, part):
        return ring(-d, facing) if part else ring(d, q)

    sibling = (row, g * 4 + q + 1 - 2 * lax.rem(q, 2))
    cross = (row, g * 4 + facing)

    def plane(step):
        return lax.rem(row + step, n_rows)

    def remote(src, dst, send, recv, device):
        return pltpu.make_async_remote_copy(
            src_ref=src, dst_ref=dst, send_sem=send, recv_sem=recv,
            device_id=device, device_id_type=MESH,
        )

    def wait_for(ref, sem):
        pltpu.make_async_copy(ref, ref, sem).wait()

    barrier = pltpu.get_barrier_semaphore()
    partners = [reader(d, part) for d, part in readers]
    partners += [ring(-d, q) for d in (1, 2, 3)]
    partners += [sibling, cross]
    partners += [(plane(j), col) for j in range(1, n_rows)]
    for device in partners:
        pl.semaphore_signal(barrier, inc=1, device_id=device, device_id_type=MESH)

    piece = quarter // 2
    side = width // 2

    def given(k):
        if k < 4:
            return (gate_hbm, up_hbm)[k // 2].at[0, 0, 0, pl.ds(k % 2 * piece, piece)]
        return down_hbm.at[0, 0, 0, :, pl.ds((k - 4) * side, side)]

    def kept(k, place):
        if k < 4:
            return (gw, uw)[k // 2].at[pl.ds(place * quarter + k % 2 * piece, piece)]
        return dw.at[k - 4, pl.ds(place * quarter, quarter)]

    local_copies = [pltpu.make_async_copy(given(k), kept(k, 0), w_local.at[k]) for k in range(6)]
    for copy in local_copies:
        copy.start()

    name = iota((experts, tokens), 0)
    hot = jnp.zeros((experts, tokens), F32)
    mix = jnp.zeros((experts, tokens), F32)
    for j in range(topk):
        same = ids_ref[j : j + 1, :] == name
        hot = hot + jnp.where(same, 1.0, 0.0)
        mix = mix + jnp.where(same, wts_ref[j : j + 1, :].astype(F32), 0.0)
    before = jnp.where(iota((tokens, tokens), 0) < iota((tokens, tokens), 1), 1.0, 0.0).astype(BF)
    earlier = nn(hot.astype(BF), before)
    order = iota((experts, experts), 0)
    slot_of = lax.rem(order, n_rows) * RING + lax.div(order, n_rows)
    pick = jnp.where(place_ref[...] == slot_of, 1.0, 0.0).astype(BF)
    place_to = nn(pick, (hot * (earlier + 1.0)).astype(BF))
    meta_out[:, :, :tokens] = place_to.reshape(RING, n_rows, tokens)
    meta_out[:, :, tokens:] = nn(pick, mix.astype(BF)).reshape(RING, n_rows, tokens)
    tok[0] = tok_ref[...]

    pl.semaphore_wait(barrier, len(partners))

    own_copies = [
        remote(tok.at[0], tok.at[1], tok_send.at[0], tok_recv.at[1], down),
        remote(tok.at[0], tok.at[2], tok_send.at[7], tok_recv.at[2], across),
    ]
    meta_copies = []
    for slot, (d, part) in enumerate(readers, 1):
        there = lax.rem(g + RING + way * (-d if part else d), RING)
        meta_copies.append(
            remote(meta_out.at[there], meta.at[slot], meta_send.at[slot], meta_recv.at[slot], reader(d, part))
        )
    for copy in meta_copies + own_copies:
        copy.start()
    meta[0] = meta_out[g]
    cross_copies = [remote(given(k), kept(k, 2), w_send.at[k], w_cross.at[k], cross) for k in range(6)]
    sib_copies = [remote(given(k), kept(k, 1), w_send.at[6 + k], w_sib.at[k], sibling) for k in range(6)]
    diag_copies = [remote(kept(k, 2), kept(k, 3), w_send.at[12 + k], w_diag.at[k], sibling) for k in range(6)]
    cross_copies[0].start()

    grow = jnp.where(lax.div(iota((slots, n_rows), 0), CAP) == iota((slots, n_rows), 1), 1.0, 0.0)
    place_in = (lax.rem(iota((slots, tokens), 0), CAP) + 1).astype(F32)

    def send_rows(src, dst, send, recv):
        pltpu.make_async_copy(src.at[row], dst.at[row], recv).start()
        for j in range(1, n_rows):
            there = plane(j)
            remote(src.at[there], dst.at[row], send, recv, (there, col)).start()

    wide = min(512, side)

    def dispatch(i, _):
        @pl.when(i > 0)
        def _():
            wait_for(tok.at[i], tok_recv.at[i])
            wait_for(meta.at[i], meta_recv.at[i])

        @pl.when((i >= 1) & (i <= 5))
        def _():
            remote(tok.at[i], tok.at[i + 2], tok_send.at[i], tok_recv.at[i + 2], down).start()

        @pl.when(i == 2)
        def _():
            cross_copies[1].start()

        @pl.when(i == 5)
        def _():
            for copy in cross_copies[2:] + sib_copies:
                copy.start()

        grown = nn(grow, meta[i])
        hot_rows = jnp.where(grown[:, :tokens] == place_in, 1.0, 0.0).astype(BF)
        for n in range(0, width, wide):
            rows = nn(hot_rows, tok[i, :, n : n + wide])
            disp[i, :, :, n : n + wide] = rows.reshape(n_rows, CAP, wide).astype(BF)
        send_rows(disp.at[i], arr.at[i], disp_send.at[i], arr_recv.at[i])
        return 0

    lax.fori_loop(0, RING, dispatch, 0)

    def take(*pieces):
        for k in pieces:
            cross_copies[k].wait_recv()
            diag_copies[k].start()

    def have(*pieces):
        for k in pieces:
            local_copies[k].wait()
            sib_copies[k].wait_recv()
            diag_copies[k].wait_recv()

    hidden = gw.shape[0]
    tile = hidden // 3

    def gated(k, _):
        wait_for(arr.at[2 * k], arr_recv.at[2 * k])
        wait_for(arr.at[2 * k + 1], arr_recv.at[2 * k + 1])
        x = arr[pl.ds(2 * k, 2)].astype(F32).reshape(2 * slots, width).astype(BF)
        for h in range(0, hidden, tile):
            gate = nt(x, gw[h : h + tile, :])
            up = nt(x, uw[h : h + tile, :])
            both = (gate / (1.0 + jnp.exp(-gate)) * up).astype(BF)
            hid[pl.ds(2 * k, 2), :, h : h + tile] = both.reshape(2, slots, tile)
        return 0

    take(0, 1, 2, 3)
    have(0, 1, 2, 3)
    lax.fori_loop(0, RING // 2, gated, 0)
    take(4)
    have(4)

    def projected(h, i):
        for n in range(0, side, wide):
            y = nn(hid[i], dw[h, :, n : n + wide])
            yout[h, i, :, :, n : n + wide] = y.reshape(n_rows, CAP, wide).astype(BF)
        send_rows(yout.at[h, i], ret.at[h, i], y_send.at[h, i], ret_recv.at[h, i])

    def part(h, i, mixer, n):
        rows = ret[h, i, :, :, n : n + wide].astype(F32).reshape(slots, wide).astype(BF)
        return tn(mixer, rows)

    def summed(h, i):
        wait_for(ret.at[h, i], ret_recv.at[h, i])
        grown = nn(grow, meta[i])
        mixer = jnp.where(grown[:, :tokens] == place_in, grown[:, tokens:], 0.0).astype(BF)

        @pl.when((i >= 1) & (i <= 5))
        def _():
            wait_for(rsum.at[h, i + 1], rs_recv.at[h, i + 1])
            for n in range(0, side, wide):
                total = part(h, i, mixer, n) + rsum[h, i + 1, :, n : n + wide].astype(F32)
                stage[h, i, :, n : n + wide] = total.astype(BF)

        @pl.when(i > 5)
        def _():
            for n in range(0, side, wide):
                stage[h, i, :, n : n + wide] = part(h, i, mixer, n).astype(BF)

        @pl.when((i >= 1) & (i != 2))
        def _():
            remote(stage.at[h, i], rsum.at[h, i - 1], rs_send.at[h, i], rs_recv.at[h, i - 1], up).start()

        @pl.when(i == 2)
        def _():
            remote(stage.at[h, 2], rsum.at[h, 1], rs_send.at[h, 2], rs_recv.at[h, 1], across).start()

        @pl.when(i == 0)
        def _():
            wait_for(rsum.at[h, 0], rs_recv.at[h, 0])
            wait_for(rsum.at[h, 1], rs_recv.at[h, 1])
            for n in range(0, side, wide):
                near = rsum[h, 0, :, n : n + wide].astype(F32) + rsum[h, 1, :, n : n + wide].astype(F32)
                at = pl.multiple_of(h * side + n, wide)
                out_ref[:, pl.ds(at, wide)] = (part(h, 0, mixer, n) + near).astype(BF)

    lag = 3

    def flow(k, _):
        @pl.when(k == RING - 2)
        def _():
            take(5)

        @pl.when(k == RING)
        def _():
            have(5)

        @pl.when(k < 2 * RING)
        def _():
            projected(lax.div(k, RING), RING - 1 - lax.rem(k, RING))

        @pl.when(k >= lag)
        def _():
            summed(lax.div(k - lag, RING), RING - 1 - lax.rem(k - lag, RING))

        return 0

    lax.fori_loop(0, 2 * RING + lag, flow, 0)

    for copy in own_copies + meta_copies + cross_copies + sib_copies + diag_copies:
        copy.wait_send()

    def drain(i, _):
        wait_for(disp.at[i, pl.ds(0, n_rows - 1)], disp_send.at[i])
        for h in range(2):
            wait_for(yout.at[h, i, pl.ds(0, n_rows - 1)], y_send.at[h, i])

        @pl.when((i >= 1) & (i <= 5))
        def _():
            wait_for(tok.at[i], tok_send.at[i])

        @pl.when(i >= 1)
        def _():
            for h in range(2):
                wait_for(stage.at[h, i], rs_send.at[h, i])

        return 0

    lax.fori_loop(0, RING, drain, 0)


def on_device(n_rows, tokens, route_ids, route_weights, placement, gate_proj, up_proj, down_proj):
    count, width = tokens.shape
    quarter = gate_proj.shape[3]
    experts = placement.shape[0]
    blocks = (RING, n_rows, CAP, width)
    vmem = pl.BlockSpec(memory_space=pltpu.VMEM)
    hbm = pl.BlockSpec(memory_space=pl.ANY)
    dma = pltpu.SemaphoreType.DMA
    halves = (2, RING, n_rows, CAP, width // 2)
    scratch = [
        pltpu.VMEM((RING, count, width), BF),
        pltpu.VMEM((RING, n_rows, 2 * count), F32),
        pltpu.VMEM((RING, n_rows, 2 * count), F32),
        pltpu.VMEM(blocks, BF),
        pltpu.VMEM(blocks, BF),
        pltpu.VMEM(halves, BF),
        pltpu.VMEM(halves, BF),
        pltpu.VMEM((2, RING, count, width // 2), BF),
        pltpu.VMEM((2, RING, count, width // 2), BF),
        pltpu.VMEM((4 * quarter, width), BF),
        pltpu.VMEM((4 * quarter, width), BF),
        pltpu.VMEM((2, 4 * quarter, width // 2), BF),
        pltpu.VMEM((RING, n_rows * CAP, 4 * quarter), BF),
    ]
    scratch += [dma((RING,)) for _ in range(6)]
    scratch += [dma((2, RING)) for _ in range(4)]
    scratch += [dma((6,)), dma((18,)), dma((6,)), dma((6,)), dma((6,))]
    return pl.pallas_call(
        functools.partial(kernel, n_rows),
        out_shape=jax.ShapeDtypeStruct((count, width), BF),
        in_specs=[vmem, vmem, vmem, vmem, hbm, hbm, hbm],
        out_specs=vmem,
        scratch_shapes=scratch,
        compiler_params=pltpu.CompilerParams(
            collective_id=0, has_side_effects=True, vmem_limit_bytes=60 * 2**20
        ),
    )(
        route_ids.T,
        route_weights.T,
        placement.reshape(1, experts),
        tokens,
        gate_proj,
        up_proj,
        down_proj,
    )


def solution(mesh):
    in_specs = (
        P(("dp", "expert"), None),
        P(("dp", "expert"), None),
        P(("dp", "expert"), None),
        P(),
        P("dp", "expert", None, None, None),
        P("dp", "expert", None, None, None),
        P("dp", "expert", None, None, None),
    )
    return jax.shard_map(
        functools.partial(on_device, mesh.shape["dp"]),
        mesh=mesh,
        in_specs=in_specs,
        out_specs=P(("dp", "expert"), None),
        check_vma=False,
    )
```

```python
import functools

import jax
import jax.numpy as jnp
from jax import lax
from jax.experimental import pallas as pl
from jax.experimental.pallas import tpu as pltpu
from jax.sharding import PartitionSpec as P

CAP = 8
BF = jnp.bfloat16
F32 = jnp.float32
MESH = pl.DeviceIdType.MESH
RING = 8
CUT = 4
PARTS = (6, 10)
STRIP = 2
CUTS = 2
EARLY = (2, 2, 4, 4, 4)
LAG = 4


def nt(a, b):
    return lax.dot_general(a, b, (((1,), (1,)), ((), ())), preferred_element_type=F32)


def nn(a, b):
    return lax.dot_general(a, b, (((1,), (0,)), ((), ())), preferred_element_type=F32)


def tn(a, b):
    return lax.dot_general(a, b, (((0,), (0,)), ((), ())), preferred_element_type=F32)


def iota(shape, dim):
    return lax.broadcasted_iota(jnp.int32, shape, dim)


def kernel(
    n_rows, ids_ref, wts_ref, place_ref, tok_ref, gate_hbm, up_hbm, down_hbm, out_ref,
    tok, meta_out, meta, disp, arr, yout, ret, stage, rsum, gw, uw, dw, hid, mixers, own,
    tok_send, tok_recv, meta_send, meta_recv, disp_send, arr_recv, y_send, ret_recv,
    rs_send, rs_recv, w_local, w_send, w_cross, w_sib, w_diag,
):
    tokens, width = tok_ref.shape
    quarter = gate_hbm.shape[3]
    experts = place_ref.shape[1]
    topk = ids_ref.shape[0]
    slots = n_rows * CAP
    row = lax.axis_index("dp")
    col = lax.axis_index("expert")
    g = lax.div(col, 4)
    q = lax.rem(col, 4)

    way = 1 - 2 * lax.div(q, 2)
    facing = lax.rem(q + 2, 4)

    def ring(step, part):
        return (row, lax.rem(g + RING + way * step, RING) * 4 + part)

    down = ring(1, q)
    up = ring(-1, q)
    across = ring(-1, facing)
    readers = [(d, part) for d in (1, 2, 3) for part in (0, 1)] + [(4, 0)]

    def reader(d, part):
        return ring(-d, facing) if part else ring(d, q)

    sibling = (row, g * 4 + q + 1 - 2 * lax.rem(q, 2))
    cross = (row, g * 4 + facing)

    def plane(step):
        return lax.rem(row + step, n_rows)

    def remote(src, dst, send, recv, device):
        return pltpu.make_async_remote_copy(
            src_ref=src, dst_ref=dst, send_sem=send, recv_sem=recv,
            device_id=device, device_id_type=MESH,
        )

    def wait_for(ref, sem):
        pltpu.make_async_copy(ref, ref, sem).wait()

    barrier = pltpu.get_barrier_semaphore()
    partners = [reader(d, part) for d, part in readers]
    partners += [ring(-d, q) for d in (1, 2, 3)]
    partners += [sibling, cross]
    partners += [(plane(j), col) for j in range(1, n_rows)]
    for device in partners:
        pl.semaphore_signal(barrier, inc=1, device_id=device, device_id_type=MESH)

    piece = quarter // CUT
    spans = tuple(width * n // 16 for n in PARTS)
    starts = tuple(sum(spans[:h]) for h in range(len(spans)))
    strip = width * STRIP // 16
    pieces = 2 * CUT + width // strip

    def given(k):
        if k < 2 * CUT:
            return (gate_hbm, up_hbm)[k // CUT].at[0, 0, 0, pl.ds(k % CUT * piece, piece)]
        return down_hbm.at[0, 0, 0, :, pl.ds((k - 2 * CUT) * strip, strip)]

    def kept(k, place):
        if k < 2 * CUT:
            return (gw, uw)[k // CUT].at[pl.ds(place * quarter + k % CUT * piece, piece)]
        return dw.at[pl.ds(place * quarter, quarter), pl.ds((k - 2 * CUT) * strip, strip)]

    local_copies = [pltpu.make_async_copy(given(k), kept(k, 0), w_local.at[k]) for k in range(pieces)]
    for copy in local_copies:
        copy.start()

    name = iota((experts, tokens), 0)
    hot = jnp.zeros((experts, tokens), F32)
    mix = jnp.zeros((experts, tokens), F32)
    for j in range(topk):
        same = ids_ref[j : j + 1, :] == name
        hot = hot + jnp.where(same, 1.0, 0.0)
        mix = mix + jnp.where(same, wts_ref[j : j + 1, :].astype(F32), 0.0)
    before = jnp.where(iota((tokens, tokens), 0) < iota((tokens, tokens), 1), 1.0, 0.0).astype(BF)
    earlier = nn(hot.astype(BF), before)
    order = iota((experts, experts), 0)
    slot_of = lax.rem(order, n_rows) * RING + lax.div(order, n_rows)
    pick = jnp.where(place_ref[...] == slot_of, 1.0, 0.0).astype(BF)
    place_to = nn(pick, (hot * (earlier + 1.0)).astype(BF))
    meta_out[:, :, :tokens] = place_to.reshape(RING, n_rows, tokens)
    meta_out[:, :, tokens:] = nn(pick, mix.astype(BF)).reshape(RING, n_rows, tokens)
    tok[0] = tok_ref[...]

    pl.semaphore_wait(barrier, len(partners))

    rows_in = tokens // CUTS

    def block(src, dst, n, send, device):
        at = pl.ds(n * rows_in, rows_in)
        return remote(tok.at[src, at], tok.at[dst, at], tok_send.at[send, n], tok_recv.at[dst, n], device)

    own_copies = []
    for n in range(CUTS):
        own_copies += [block(0, 1, n, 0, down), block(0, 2, n, 7, across)]
    meta_copies = []
    for slot, (d, part) in enumerate(readers, 1):
        there = lax.rem(g + RING + way * (-d if part else d), RING)
        meta_copies.append(
            remote(meta_out.at[there], meta.at[slot], meta_send.at[slot], meta_recv.at[slot], reader(d, part))
        )
    for copy in meta_copies + own_copies:
        copy.start()
    meta[0] = meta_out[g]
    cross_copies = [remote(given(k), kept(k, 2), w_send.at[k], w_cross.at[k], cross) for k in range(pieces)]
    sib_copies = [remote(given(k), kept(k, 1), w_send.at[pieces + k], w_sib.at[k], sibling) for k in range(pieces)]
    diag_copies = [remote(kept(k, 2), kept(k, 3), w_send.at[2 * pieces + k], w_diag.at[k], sibling) for k in range(pieces)]
    for k in range(EARLY[0]):
        cross_copies[k].start()

    grow = jnp.where(lax.div(iota((slots, n_rows), 0), CAP) == iota((slots, n_rows), 1), 1.0, 0.0)
    place_in = (lax.rem(iota((slots, tokens), 0), CAP) + 1).astype(F32)

    def send_rows(src, dst, send, recv):
        pltpu.make_async_copy(src.at[row], dst.at[row], recv).start()
        for j in range(1, n_rows):
            there = plane(j)
            remote(src.at[there], dst.at[row], send, recv, (there, col)).start()

    wide = min(512, strip)
    assert all(n % strip == 0 for n in spans)

    def dispatch(i, _):
        def arrive(slot, n):
            wait_for(tok.at[slot, pl.ds(n * rows_in, rows_in)], tok_recv.at[slot, n])

        @pl.when((i == 1) | (i == 3))
        def _():
            for n in range(CUTS):
                for slot in (i, i + 1):
                    arrive(slot, n)
                    block(slot, slot + 2, n, slot, down).start()

        @pl.when(i == 5)
        def _():
            for n in range(CUTS):
                arrive(5, n)
                block(5, 7, n, 5, down).start()

        @pl.when(i >= 6)
        def _():
            for n in range(CUTS):
                arrive(i, n)

        @pl.when(i > 0)
        def _():
            wait_for(meta.at[i], meta_recv.at[i])

        for step in range(1, 5):
            if EARLY[step] > EARLY[step - 1]:

                @pl.when(i == step)
                def _():
                    for k in range(EARLY[step - 1], EARLY[step]):
                        cross_copies[k].start()

        @pl.when(i == 5)
        def _():
            for copy in cross_copies[EARLY[4] :] + sib_copies:
                copy.start()

        grown = nn(grow, meta[i])
        hot_rows = jnp.where(grown[:, :tokens] == place_in, 1.0, 0.0).astype(BF)
        for n in range(0, width, wide):
            rows = nn(hot_rows, tok[i, :, n : n + wide])
            disp[i, :, :, n : n + wide] = rows.reshape(n_rows, CAP, wide).astype(BF)
        send_rows(disp.at[i], arr.at[i], disp_send.at[i], arr_recv.at[i])
        return 0

    lax.fori_loop(0, RING, dispatch, 0)

    def take(*pieces):
        for k in pieces:
            cross_copies[k].wait_recv()
            diag_copies[k].start()

    def have(*pieces):
        for k in pieces:
            local_copies[k].wait()
            sib_copies[k].wait_recv()
            diag_copies[k].wait_recv()

    hidden = gw.shape[0]
    tile = hidden // 3

    def gated(k, _):
        wait_for(arr.at[2 * k], arr_recv.at[2 * k])
        wait_for(arr.at[2 * k + 1], arr_recv.at[2 * k + 1])
        x = arr[pl.ds(2 * k, 2)].astype(F32).reshape(2 * slots, width).astype(BF)
        for h in range(0, hidden, tile):
            gate = nt(x, gw[h : h + tile, :])
            up = nt(x, uw[h : h + tile, :])
            both = (gate / (1.0 + jnp.exp(-gate)) * up).astype(BF)
            hid[pl.ds(2 * k, 2), :, h : h + tile] = both.reshape(2, slots, tile)
        return 0

    eye = jnp.where(iota((slots, slots), 0) == iota((slots, slots), 1), 1.0, 0.0).astype(BF)

    def mixing(i, _):
        grown = nn(grow, meta[i])
        mixer = jnp.where(grown[:, :tokens] == place_in, grown[:, tokens:], 0.0).astype(BF)
        mixers[i] = tn(mixer, eye).astype(BF)
        return 0

    lax.fori_loop(0, RING, mixing, 0)

    take(*range(2 * CUT))
    have(*range(2 * CUT))
    lax.fori_loop(0, RING // 2, gated, 0)
    strips_of = [
        range(2 * CUT + starts[h] // strip, 2 * CUT + (starts[h] + spans[h]) // strip) for h in range(len(spans))
    ]
    take(*strips_of[0])
    have(*strips_of[0])

    def projected(h, i):
        for n in range(0, spans[h], wide):
            y = nn(hid[i], dw[:, starts[h] + n : starts[h] + n + wide])
            yout[h][i, :, :, n : n + wide] = y.reshape(n_rows, CAP, wide).astype(BF)
        send_rows(yout[h].at[i], ret[h].at[i], y_send.at[h, i], ret_recv.at[h, i])

    def part(h, i, n):
        rows = ret[h][i, :, :, n : n + wide].astype(F32).reshape(slots, wide).astype(BF)
        return nn(mixers[i], rows)

    def summed(h, i):
        wait_for(ret[h].at[i], ret_recv.at[h, i])

        @pl.when((i >= 1) & (i <= 5))
        def _():
            wait_for(rsum[h].at[i + 1], rs_recv.at[h, i + 1])
            for n in range(0, spans[h], wide):
                total = part(h, i, n) + rsum[h][i + 1, :, n : n + wide].astype(F32)
                stage[h][i, :, n : n + wide] = total.astype(BF)

        @pl.when(i > 5)
        def _():
            for n in range(0, spans[h], wide):
                stage[h][i, :, n : n + wide] = part(h, i, n).astype(BF)

        @pl.when(i == 0)
        def _():
            for n in range(0, spans[h], wide):
                own[:, starts[h] + n : starts[h] + n + wide] = part(h, 0, n)

        @pl.when((i >= 1) & (i != 2))
        def _():
            remote(stage[h].at[i], rsum[h].at[i - 1], rs_send.at[h, i], rs_recv.at[h, i - 1], up).start()

        @pl.when(i == 2)
        def _():
            remote(stage[h].at[2], rsum[h].at[1], rs_send.at[h, 2], rs_recv.at[h, 1], across).start()

    def flow(k, _):
        for h in range(1, len(spans)):
            pace = max(1, RING // 2 // len(strips_of[h]))
            for n, strip_now in enumerate(strips_of[h]):

                @pl.when(k == RING * h - pace * (len(strips_of[h]) - n))
                def _(strip_now=strip_now):
                    take(strip_now)

            @pl.when(k == RING * h)
            def _():
                have(*strips_of[h])

        for h in range(len(spans)):

            @pl.when(lax.div(k, RING) == h)
            def _():
                projected(h, RING - 1 - lax.rem(k, RING))

        for h in range(len(spans)):

            @pl.when(lax.div(k + RING - LAG, RING) == h + 1)
            def _():
                summed(h, RING - 1 - lax.rem(k + RING - LAG, RING))

        return 0

    lax.fori_loop(0, len(spans) * RING + LAG, flow, 0)

    for h in range(len(spans)):
        wait_for(rsum[h].at[0], rs_recv.at[h, 0])
        wait_for(rsum[h].at[1], rs_recv.at[h, 1])
        at = pl.ds(starts[h], spans[h])
        out_ref[:, at] = (own[:, at] + rsum[h][0].astype(F32) + rsum[h][1].astype(F32)).astype(BF)

    for copy in own_copies + meta_copies + cross_copies + sib_copies + diag_copies:
        copy.wait_send()

    def drain(i, _):
        wait_for(disp.at[i, pl.ds(0, n_rows - 1)], disp_send.at[i])
        for h in range(len(spans)):
            wait_for(yout[h].at[i, pl.ds(0, n_rows - 1)], y_send.at[h, i])

        @pl.when((i >= 1) & (i <= 5))
        def _():
            for n in range(CUTS):
                wait_for(tok.at[i, pl.ds(n * rows_in, rows_in)], tok_send.at[i, n])

        @pl.when(i >= 1)
        def _():
            for h in range(len(spans)):
                wait_for(stage[h].at[i], rs_send.at[h, i])

        return 0

    lax.fori_loop(0, RING, drain, 0)


def on_device(n_rows, tokens, route_ids, route_weights, placement, gate_proj, up_proj, down_proj):
    count, width = tokens.shape
    quarter = gate_proj.shape[3]
    experts = placement.shape[0]
    blocks = (RING, n_rows, CAP, width)
    vmem = pl.BlockSpec(memory_space=pltpu.VMEM)
    hbm = pl.BlockSpec(memory_space=pl.ANY)
    dma = pltpu.SemaphoreType.DMA
    spans = tuple(width * n // 16 for n in PARTS)
    parted = tuple(pltpu.VMEM((RING, n_rows, CAP, n), BF) for n in spans)
    summing = tuple(pltpu.VMEM((RING, count, n), BF) for n in spans)
    scratch = [
        pltpu.VMEM((RING, count, width), BF),
        pltpu.VMEM((RING, n_rows, 2 * count), F32),
        pltpu.VMEM((RING, n_rows, 2 * count), F32),
        pltpu.VMEM(blocks, BF),
        pltpu.VMEM(blocks, BF),
        parted,
        parted,
        summing,
        summing,
        pltpu.VMEM((4 * quarter, width), BF),
        pltpu.VMEM((4 * quarter, width), BF),
        pltpu.VMEM((4 * quarter, width), BF),
        pltpu.VMEM((RING, n_rows * CAP, 4 * quarter), BF),
        pltpu.VMEM((RING, count, n_rows * CAP), BF),
        pltpu.VMEM((count, width), F32),
    ]
    scratch += [dma((RING, CUTS)) for _ in range(2)]
    scratch += [dma((RING,)) for _ in range(4)]
    scratch += [dma((len(PARTS), RING)) for _ in range(4)]
    pieces = 2 * CUT + 16 // STRIP
    scratch += [dma((pieces,)), dma((3 * pieces,)), dma((pieces,)), dma((pieces,)), dma((pieces,))]
    return pl.pallas_call(
        functools.partial(kernel, n_rows),
        out_shape=jax.ShapeDtypeStruct((count, width), BF),
        in_specs=[vmem, vmem, vmem, vmem, hbm, hbm, hbm],
        out_specs=vmem,
        scratch_shapes=scratch,
        compiler_params=pltpu.CompilerParams(
            collective_id=0, has_side_effects=True, vmem_limit_bytes=60 * 2**20
        ),
    )(
        route_ids.T,
        route_weights.T,
        placement.reshape(1, experts),
        tokens,
        gate_proj,
        up_proj,
        down_proj,
    )


def solution(mesh):
    in_specs = (
        P(("dp", "expert"), None),
        P(("dp", "expert"), None),
        P(("dp", "expert"), None),
        P(),
        P("dp", "expert", None, None, None),
        P("dp", "expert", None, None, None),
        P("dp", "expert", None, None, None),
    )
    return jax.shard_map(
        functools.partial(on_device, mesh.shape["dp"]),
        mesh=mesh,
        in_specs=in_specs,
        out_specs=P(("dp", "expert"), None),
        check_vma=False,
    )
```

```python
import functools

import jax
import jax.numpy as jnp
from jax import lax
from jax.experimental import pallas as pl
from jax.experimental.pallas import tpu as pltpu
from jax.sharding import PartitionSpec as P

CAP = 8
BF = jnp.bfloat16
F32 = jnp.float32
MESH = pl.DeviceIdType.MESH
RING = 8
CUT = 4
PARTS = (6, 10)
STRIP = 2
CUTS = 2
EARLY = (2, 2, 4, 4, 4)
LAG = 6


def nt(a, b):
    return lax.dot_general(a, b, (((1,), (1,)), ((), ())), preferred_element_type=F32)


def nn(a, b):
    return lax.dot_general(a, b, (((1,), (0,)), ((), ())), preferred_element_type=F32)


def tn(a, b):
    return lax.dot_general(a, b, (((0,), (0,)), ((), ())), preferred_element_type=F32)


def iota(shape, dim):
    return lax.broadcasted_iota(jnp.int32, shape, dim)


def kernel(
    n_rows, ids_ref, wts_ref, place_ref, tok_ref, gate_hbm, up_hbm, down_hbm, out_ref,
    tok, meta_out, meta, disp, arr, yout, ret, stage, rsum, gw, uw, dw, hid, mixers, own,
    tok_send, tok_recv, meta_send, meta_recv, disp_send, arr_recv, y_send, ret_recv,
    rs_send, rs_recv, w_local, w_send, w_cross, w_sib, w_diag,
):
    tokens, width = tok_ref.shape
    quarter = gate_hbm.shape[3]
    experts = place_ref.shape[1]
    topk = ids_ref.shape[0]
    slots = n_rows * CAP
    row = lax.axis_index("dp")
    col = lax.axis_index("expert")
    g = lax.div(col, 4)
    q = lax.rem(col, 4)

    way = 1 - 2 * lax.div(q, 2)
    facing = lax.rem(q + 2, 4)

    def ring(step, part):
        return (row, lax.rem(g + RING + way * step, RING) * 4 + part)

    down = ring(1, q)
    up = ring(-1, q)
    across = ring(-1, facing)
    readers = [(d, part) for d in (1, 2, 3) for part in (0, 1)] + [(4, 0)]

    def reader(d, part):
        return ring(-d, facing) if part else ring(d, q)

    sibling = (row, g * 4 + q + 1 - 2 * lax.rem(q, 2))
    cross = (row, g * 4 + facing)

    def plane(step):
        return lax.rem(row + step, n_rows)

    def remote(src, dst, send, recv, device):
        return pltpu.make_async_remote_copy(
            src_ref=src, dst_ref=dst, send_sem=send, recv_sem=recv,
            device_id=device, device_id_type=MESH,
        )

    def wait_for(ref, sem):
        pltpu.make_async_copy(ref, ref, sem).wait()

    barrier = pltpu.get_barrier_semaphore()
    partners = [reader(d, part) for d, part in readers]
    partners += [ring(-d, q) for d in (1, 2, 3)]
    partners += [sibling, cross]
    partners += [(plane(j), col) for j in range(1, n_rows)]
    for device in partners:
        pl.semaphore_signal(barrier, inc=1, device_id=device, device_id_type=MESH)

    piece = quarter // CUT
    spans = tuple(width * n // 16 for n in PARTS)
    starts = tuple(sum(spans[:h]) for h in range(len(spans)))
    strip = width * STRIP // 16
    pieces = 2 * CUT + width // strip

    def given(k):
        if k < 2 * CUT:
            return (gate_hbm, up_hbm)[k // CUT].at[0, 0, 0, pl.ds(k % CUT * piece, piece)]
        return down_hbm.at[0, 0, 0, :, pl.ds((k - 2 * CUT) * strip, strip)]

    def kept(k, place):
        if k < 2 * CUT:
            return (gw, uw)[k // CUT].at[pl.ds(place * quarter + k % CUT * piece, piece)]
        return dw.at[pl.ds(place * quarter, quarter), pl.ds((k - 2 * CUT) * strip, strip)]

    local_copies = [pltpu.make_async_copy(given(k), kept(k, 0), w_local.at[k]) for k in range(pieces)]
    for copy in local_copies:
        copy.start()

    name = iota((experts, tokens), 0)
    hot = jnp.zeros((experts, tokens), F32)
    mix = jnp.zeros((experts, tokens), F32)
    for j in range(topk):
        same = ids_ref[j : j + 1, :] == name
        hot = hot + jnp.where(same, 1.0, 0.0)
        mix = mix + jnp.where(same, wts_ref[j : j + 1, :].astype(F32), 0.0)
    before = jnp.where(iota((tokens, tokens), 0) < iota((tokens, tokens), 1), 1.0, 0.0).astype(BF)
    earlier = nn(hot.astype(BF), before)
    order = iota((experts, experts), 0)
    slot_of = lax.rem(order, n_rows) * RING + lax.div(order, n_rows)
    pick = jnp.where(place_ref[...] == slot_of, 1.0, 0.0).astype(BF)
    place_to = nn(pick, (hot * (earlier + 1.0)).astype(BF))
    meta_out[:, :, :tokens] = place_to.reshape(RING, n_rows, tokens)
    meta_out[:, :, tokens:] = nn(pick, mix.astype(BF)).reshape(RING, n_rows, tokens)
    tok[0] = tok_ref[...]

    pl.semaphore_wait(barrier, len(partners))

    rows_in = tokens // CUTS

    def block(src, dst, n, send, device):
        at = pl.ds(n * rows_in, rows_in)
        return remote(tok.at[src, at], tok.at[dst, at], tok_send.at[send, n], tok_recv.at[dst, n], device)

    own_copies = []
    for n in range(CUTS):
        own_copies += [block(0, 1, n, 0, down), block(0, 2, n, 7, across)]
    meta_copies = []
    for slot, (d, part) in enumerate(readers, 1):
        there = lax.rem(g + RING + way * (-d if part else d), RING)
        meta_copies.append(
            remote(meta_out.at[there], meta.at[slot], meta_send.at[slot], meta_recv.at[slot], reader(d, part))
        )
    for copy in meta_copies + own_copies:
        copy.start()
    meta[0] = meta_out[g]
    cross_copies = [remote(given(k), kept(k, 2), w_send.at[k], w_cross.at[k], cross) for k in range(pieces)]
    sib_copies = [remote(given(k), kept(k, 1), w_send.at[pieces + k], w_sib.at[k], sibling) for k in range(pieces)]
    diag_copies = [remote(kept(k, 2), kept(k, 3), w_send.at[2 * pieces + k], w_diag.at[k], sibling) for k in range(pieces)]
    for k in range(EARLY[0]):
        cross_copies[k].start()

    grow = jnp.where(lax.div(iota((slots, n_rows), 0), CAP) == iota((slots, n_rows), 1), 1.0, 0.0)
    place_in = (lax.rem(iota((slots, tokens), 0), CAP) + 1).astype(F32)

    def send_rows(src, dst, send, recv):
        pltpu.make_async_copy(src.at[row], dst.at[row], recv).start()
        for j in range(1, n_rows):
            there = plane(j)
            remote(src.at[there], dst.at[row], send, recv, (there, col)).start()

    wide = min(512, strip)
    assert all(n % strip == 0 for n in spans)

    def dispatch(i, _):
        def arrive(slot, n):
            wait_for(tok.at[slot, pl.ds(n * rows_in, rows_in)], tok_recv.at[slot, n])

        @pl.when((i == 1) | (i == 3))
        def _():
            for n in range(CUTS):
                for slot in (i, i + 1):
                    arrive(slot, n)
                    block(slot, slot + 2, n, slot, down).start()

        @pl.when(i == 5)
        def _():
            for n in range(CUTS):
                arrive(5, n)
                block(5, 7, n, 5, down).start()

        @pl.when(i >= 6)
        def _():
            for n in range(CUTS):
                arrive(i, n)

        @pl.when(i > 0)
        def _():
            wait_for(meta.at[i], meta_recv.at[i])

        for step in range(1, 5):
            if EARLY[step] > EARLY[step - 1]:

                @pl.when(i == step)
                def _():
                    for k in range(EARLY[step - 1], EARLY[step]):
                        cross_copies[k].start()

        @pl.when(i == 5)
        def _():
            for copy in cross_copies[EARLY[4] :] + sib_copies:
                copy.start()

        grown = nn(grow, meta[i])
        hot_rows = jnp.where(grown[:, :tokens] == place_in, 1.0, 0.0).astype(BF)
        for n in range(0, width, wide):
            rows = nn(hot_rows, tok[i, :, n : n + wide])
            disp[i, :, :, n : n + wide] = rows.reshape(n_rows, CAP, wide).astype(BF)
        send_rows(disp.at[i], arr.at[i], disp_send.at[i], arr_recv.at[i])
        return 0

    lax.fori_loop(0, RING, dispatch, 0)

    def take(*pieces):
        for k in pieces:
            cross_copies[k].wait_recv()
            diag_copies[k].start()

    def have(*pieces):
        for k in pieces:
            local_copies[k].wait()
            sib_copies[k].wait_recv()
            diag_copies[k].wait_recv()

    hidden = gw.shape[0]
    tile = hidden // 3

    def gated(k, _):
        wait_for(arr.at[2 * k], arr_recv.at[2 * k])
        wait_for(arr.at[2 * k + 1], arr_recv.at[2 * k + 1])
        x = arr[pl.ds(2 * k, 2)].astype(F32).reshape(2 * slots, width).astype(BF)
        for h in range(0, hidden, tile):
            gate = nt(x, gw[h : h + tile, :])
            up = nt(x, uw[h : h + tile, :])
            both = (gate / (1.0 + jnp.exp(-gate)) * up).astype(BF)
            hid[pl.ds(2 * k, 2), :, h : h + tile] = both.reshape(2, slots, tile)
        return 0

    eye = jnp.where(iota((slots, slots), 0) == iota((slots, slots), 1), 1.0, 0.0).astype(BF)

    def mixing(i, _):
        grown = nn(grow, meta[i])
        mixer = jnp.where(grown[:, :tokens] == place_in, grown[:, tokens:], 0.0).astype(BF)
        mixers[i] = tn(mixer, eye).astype(BF)
        return 0

    lax.fori_loop(0, RING, mixing, 0)

    take(*range(2 * CUT))
    have(*range(2 * CUT))
    lax.fori_loop(0, RING // 2, gated, 0)
    strips_of = [
        range(2 * CUT + starts[h] // strip, 2 * CUT + (starts[h] + spans[h]) // strip) for h in range(len(spans))
    ]
    take(*strips_of[0])
    have(*strips_of[0])

    def projected(h, i):
        for n in range(0, spans[h], wide):
            y = nn(hid[i], dw[:, starts[h] + n : starts[h] + n + wide])
            yout[h][i, :, :, n : n + wide] = y.reshape(n_rows, CAP, wide).astype(BF)
        send_rows(yout[h].at[i], ret[h].at[i], y_send.at[h, i], ret_recv.at[h, i])

    def part(h, i, n):
        rows = ret[h][i, :, :, n : n + wide].astype(F32).reshape(slots, wide).astype(BF)
        return nn(mixers[i], rows)

    def summed(h, i):
        wait_for(ret[h].at[i], ret_recv.at[h, i])

        @pl.when((i >= 1) & (i <= 5))
        def _():
            wait_for(rsum[h].at[i + 1], rs_recv.at[h, i + 1])
            for n in range(0, spans[h], wide):
                total = part(h, i, n) + rsum[h][i + 1, :, n : n + wide].astype(F32)
                stage[h][i, :, n : n + wide] = total.astype(BF)

        @pl.when(i > 5)
        def _():
            for n in range(0, spans[h], wide):
                stage[h][i, :, n : n + wide] = part(h, i, n).astype(BF)

        @pl.when(i == 0)
        def _():
            for n in range(0, spans[h], wide):
                own[:, starts[h] + n : starts[h] + n + wide] = part(h, 0, n)

        @pl.when((i >= 1) & (i != 2))
        def _():
            remote(stage[h].at[i], rsum[h].at[i - 1], rs_send.at[h, i], rs_recv.at[h, i - 1], up).start()

        @pl.when(i == 2)
        def _():
            remote(stage[h].at[2], rsum[h].at[1], rs_send.at[h, 2], rs_recv.at[h, 1], across).start()

    def flow(k, _):
        for h in range(1, len(spans)):
            pace = max(1, RING // 2 // len(strips_of[h]))
            for n, strip_now in enumerate(strips_of[h]):

                @pl.when(k == RING * h - pace * (len(strips_of[h]) - n))
                def _(strip_now=strip_now):
                    take(strip_now)

            @pl.when(k == RING * h)
            def _():
                have(*strips_of[h])

        for h in range(len(spans)):

            @pl.when(lax.div(k, RING) == h)
            def _():
                projected(h, RING - 1 - lax.rem(k, RING))

        for h in range(len(spans)):

            @pl.when(lax.div(k + RING - LAG, RING) == h + 1)
            def _():
                summed(h, RING - 1 - lax.rem(k + RING - LAG, RING))

        return 0

    lax.fori_loop(0, len(spans) * RING + LAG, flow, 0)

    for h in range(len(spans)):
        wait_for(rsum[h].at[0], rs_recv.at[h, 0])
        wait_for(rsum[h].at[1], rs_recv.at[h, 1])
        at = pl.ds(starts[h], spans[h])
        out_ref[:, at] = (own[:, at] + rsum[h][0].astype(F32) + rsum[h][1].astype(F32)).astype(BF)

    for copy in own_copies + meta_copies + cross_copies + sib_copies + diag_copies:
        copy.wait_send()

    def drain(i, _):
        wait_for(disp.at[i, pl.ds(0, n_rows - 1)], disp_send.at[i])
        for h in range(len(spans)):
            wait_for(yout[h].at[i, pl.ds(0, n_rows - 1)], y_send.at[h, i])

        @pl.when((i >= 1) & (i <= 5))
        def _():
            for n in range(CUTS):
                wait_for(tok.at[i, pl.ds(n * rows_in, rows_in)], tok_send.at[i, n])

        @pl.when(i >= 1)
        def _():
            for h in range(len(spans)):
                wait_for(stage[h].at[i], rs_send.at[h, i])

        return 0

    lax.fori_loop(0, RING, drain, 0)


def on_device(n_rows, tokens, route_ids, route_weights, placement, gate_proj, up_proj, down_proj):
    count, width = tokens.shape
    quarter = gate_proj.shape[3]
    experts = placement.shape[0]
    blocks = (RING, n_rows, CAP, width)
    vmem = pl.BlockSpec(memory_space=pltpu.VMEM)
    hbm = pl.BlockSpec(memory_space=pl.ANY)
    dma = pltpu.SemaphoreType.DMA
    spans = tuple(width * n // 16 for n in PARTS)
    parted = tuple(pltpu.VMEM((RING, n_rows, CAP, n), BF) for n in spans)
    summing = tuple(pltpu.VMEM((RING, count, n), BF) for n in spans)
    scratch = [
        pltpu.VMEM((RING, count, width), BF),
        pltpu.VMEM((RING, n_rows, 2 * count), F32),
        pltpu.VMEM((RING, n_rows, 2 * count), F32),
        pltpu.VMEM(blocks, BF),
        pltpu.VMEM(blocks, BF),
        parted,
        parted,
        summing,
        summing,
        pltpu.VMEM((4 * quarter, width), BF),
        pltpu.VMEM((4 * quarter, width), BF),
        pltpu.VMEM((4 * quarter, width), BF),
        pltpu.VMEM((RING, n_rows * CAP, 4 * quarter), BF),
        pltpu.VMEM((RING, count, n_rows * CAP), BF),
        pltpu.VMEM((count, width), F32),
    ]
    scratch += [dma((RING, CUTS)) for _ in range(2)]
    scratch += [dma((RING,)) for _ in range(4)]
    scratch += [dma((len(PARTS), RING)) for _ in range(4)]
    pieces = 2 * CUT + 16 // STRIP
    scratch += [dma((pieces,)), dma((3 * pieces,)), dma((pieces,)), dma((pieces,)), dma((pieces,))]
    return pl.pallas_call(
        functools.partial(kernel, n_rows),
        out_shape=jax.ShapeDtypeStruct((count, width), BF),
        in_specs=[vmem, vmem, vmem, vmem, hbm, hbm, hbm],
        out_specs=vmem,
        scratch_shapes=scratch,
        compiler_params=pltpu.CompilerParams(
            collective_id=0, has_side_effects=True, vmem_limit_bytes=60 * 2**20
        ),
    )(
        route_ids.T,
        route_weights.T,
        placement.reshape(1, experts),
        tokens,
        gate_proj,
        up_proj,
        down_proj,
    )


def solution(mesh):
    in_specs = (
        P(("dp", "expert"), None),
        P(("dp", "expert"), None),
        P(("dp", "expert"), None),
        P(),
        P("dp", "expert", None, None, None),
        P("dp", "expert", None, None, None),
        P("dp", "expert", None, None, None),
    )
    return jax.shard_map(
        functools.partial(on_device, mesh.shape["dp"]),
        mesh=mesh,
        in_specs=in_specs,
        out_specs=P(("dp", "expert"), None),
        check_vma=False,
    )
```
